32 devices in a mesh: ep: 4 (over y, x), dp: 8 (over z, core).
Axes of the slice: x: 2, y: 2, z: 4, core: 2. Of those that a mesh axis runs over, the one named last changes fastest.
Arguments:
- checkpoint: bfloat16 [4096, 2048], P('ep', 'dp'), may hold values from -6 to 6
- cotangent: bfloat16 [4096, 2048], P(('ep', 'dp')), may hold values from -6 to 6
- routes: int32 [4096, 2], P(('ep', 'dp')), may hold values from 0 to 3, all different within a row; in each aligned block of 128 rows (0 to 127, 128 to 255, ...) at most 128 rows name the same one
- gates: float32 [4096, 2], P(('ep', 'dp')), may hold values from 0.1 to 1
- w_gate: bfloat16 [4, 2048, 1024], P('ep'), may hold values from -0.125 to 0.125
- w_up: bfloat16 [4, 2048, 1024], P('ep'), may hold values from -0.125 to 0.125
- w_down: bfloat16 [4, 2048, 1024], P('ep'), may hold values from -0.1875 to 0.1875
Outputs:
- layer_out: bfloat16 [4096, 2048], P(('ep', 'dp'))
- grad_input: bfloat16 [4096, 2048], P(('ep', 'dp'))
- grad_gates: float32 [4096, 2], P(('ep', 'dp'))
- grad_w_gate: float32 [4, 2048, 1024], P('ep', 'dp')
- grad_w_up: float32 [4, 2048, 1024], P('ep', 'dp')
- grad_w_down: float32 [4, 2048, 1024], P('ep', 'dp')
The draws below stay inside these ranges and needn't reach their ends.
Inputs may be any that keep to these rules, and one draw needn't show every extreme that they name: `routes`: among the 128 rows of one device, no expert is named by more than 128 rows, and in every draw some expert is named by exactly 128 of them; a token names 2 different experts.
All inputs are finite; a program needn't handle non-finite values.
Results may differ from the reference program's by a relative error of at most 0.022.
Values may be sent and summed in bfloat16 or wider, within the bound.
A program may use at most 128 MiB of HBM per device.

```python
import math
import jax
import jax.numpy as jnp
import numpy as np
from jax import lax

D = 2048
FF = 1024
TOP = 2
TOK_DEV = 128
EXPERTS = 4
CAP = 128
TOKENS = 4096
DEVICES = 32


def level_of(own_key, extent, split, smallest, largest):
    gain = 1.0
    for dim, blocks in split:
        heights = jax.random.uniform(jax.random.fold_in(jax.random.fold_in(own_key, 6), dim), (blocks,), jnp.float32, smallest / len(split), largest / len(split))
        gain = gain * jnp.repeat(jnp.exp(heights), extent[dim] // blocks).reshape((-1,) + (1,) * (len(extent) - 1 - dim))
    return gain


def routed_block(key, own, number, rows, amount, top, reach, lean):
    sequence = jax.random.permutation(key, amount)
    heavy_load, ordinary = load_shares(amount, rows * top, reach, lean, True), load_shares(amount, rows * top, reach, lean, False)
    places = jnp.arange(amount)

    def named(sizes, turn):
        used = int((sizes > 0).sum())
        fixed = max(1, used // 4)
        shifted = fixed + (places - fixed + turn * (used - fixed)) % max(1, amount - fixed)
        return jnp.zeros((amount,), jnp.int32).at[sequence[jnp.where(places < fixed, places, shifted)]].set(jnp.asarray(sizes, jnp.int32))

    sizes = jnp.where(number % 4 == 0, named(heavy_load, number // 4), named(ordinary, number - number // 4 - 1))
    mixed = jax.random.permutation(jax.random.fold_in(own, 3), amount)
    source_of, taker = mixed[0:amount // 2 * 2:2], mixed[1:amount // 2 * 2:2]
    room = jnp.minimum(sizes[source_of] - 1, reach - sizes[taker]) // 2
    room = jnp.where((source_of == sequence[0]) | (taker == sequence[0]) | (sizes[taker] == 0), 0, jnp.maximum(room, 0))
    shifted = jax.random.randint(jax.random.fold_in(own, 4), (amount // 2,), 0, 1 << 20) % (room + 1)
    sizes = sizes.at[source_of].add(-shifted).at[taker].add(shifted)
    items = jnp.searchsorted(jnp.cumsum(sizes), jnp.arange(rows * top), side="right").astype(jnp.int32)
    grid = items.reshape(top, rows).T
    grid = grid[jax.random.permutation(jax.random.fold_in(own, 1), rows)]
    turn = jax.random.randint(jax.random.fold_in(own, 2), (rows, 1), 0, top)
    return jnp.take_along_axis(grid, (jnp.arange(top)[None, :] + turn) % top, axis=1)


def load_shares(amount, total, most, lean, full):
    loads = [(1 << 20) // math.isqrt(standing ** lean) + 1 for standing in range(1, amount + 1)]
    largest = most if full else min(most, max(-(-total // amount), total * loads[0] // sum(loads)))
    least = 1 if total - largest >= amount - 1 else 0
    given, rest = [largest] + [least] * (amount - 1), total - largest - least * (amount - 1)
    while rest > 0:
        movable = [i for i in range(1, amount) if given[i] < largest] or [i for i in range(1, amount) if given[i] < most]
        pool, left = sum([loads[i] for i in movable]), rest
        for i in movable:
            addition = min(most - given[i], max(1, left * loads[i] // pool), rest)
            given[i] = given[i] + addition
            rest = rest - addition
    return np.array(given)


def noise(key, dims, scale, bound, shards=(), kind=jnp.bfloat16):
    loudness = level_of(key, dims, shards, -0.22, 0.18) if shards else 1.0
    values = jax.random.normal(key, dims, jnp.float32) * scale * loudness
    return jnp.minimum(jnp.maximum(values, -bound), bound).astype(kind)


def setup_inputs(seed: int = 0) -> dict:
    key_of = jax.random.split(jax.random.key(seed), 8)
    checkpoint = noise(key_of[0], (TOKENS, D), 1.0, 6.0, ((0, 4), (1, 8)))
    cotangent = noise(key_of[1], (TOKENS, D), 1.0, 6.0, ((0, 32),))
    routes_keys = jax.random.split(jax.random.fold_in(key_of[2], 1), TOKENS // TOK_DEV)
    routes_turns = jax.random.permutation(jax.random.fold_in(key_of[2], 3), TOKENS // TOK_DEV)
    routes = jax.vmap(lambda own, number: routed_block(jax.random.fold_in(key_of[2], 2), own, number, TOK_DEV, EXPERTS, TOP, CAP, 2))(routes_keys, routes_turns).reshape((TOKENS, TOP))
    gates = jnp.clip(jnp.exp(math.log(1.0) - 2.3025851 * jax.random.uniform(key_of[3], (TOKENS, TOP), jnp.float32) ** level_of(key_of[3], (TOKENS, TOP), ((0, 32),), -0.2, 0.2)), 0.1, 1.0)
    w_gate = noise(key_of[4], (EXPERTS, D, FF), D ** -0.5, 0.125, ((0, 4),))
    w_up = noise(key_of[5], (EXPERTS, D, FF), D ** -0.5, 0.125, ((0, 4),))
    w_down = noise(key_of[6], (EXPERTS, D, FF), FF ** -0.5, 0.1875, ((0, 4),))
    return {"checkpoint": checkpoint, "cotangent": cotangent, "routes": routes, "gates": gates, "w_gate": w_gate, "w_up": w_up, "w_down": w_down}


def reference(checkpoint, cotangent, routes, gates, w_gate, w_up, w_down):
    pair_count = TOKENS * TOP
    flat_routes = routes.reshape(-1).astype(jnp.int32)
    one_hot = (flat_routes[:, None] == jnp.arange(EXPERTS, dtype=jnp.int32)[None, :]).astype(jnp.int32)
    blocks = one_hot.reshape(DEVICES, TOK_DEV * TOP, EXPERTS)
    slot_index = (jnp.sum(jnp.cumsum(blocks, axis=1) * blocks, axis=2) - 1).reshape(-1)
    device_index = jnp.arange(pair_count, dtype=jnp.int32) // (TOK_DEV * TOP)
    position = (device_index * CAP + slot_index).astype(jnp.int32)
    source = jnp.full((EXPERTS, DEVICES * CAP), pair_count, jnp.int32)
    source = source.at[flat_routes, position].set(jnp.arange(pair_count, dtype=jnp.int32))
    x_padded = jnp.concatenate([checkpoint, jnp.zeros((1, D), jnp.bfloat16)], axis=0)
    grad_out = (gates[:, :, None] * cotangent[:, None, :].astype(jnp.float32)).astype(jnp.bfloat16)
    grad_padded = jnp.concatenate([grad_out.reshape(pair_count, D), jnp.zeros((1, D), jnp.bfloat16)], axis=0)

    def expert(operands):
        gate_w, up_w, down_w, rows_source = operands
        token_index = jnp.minimum(rows_source // TOP, TOKENS)
        x_rows = x_padded[token_index]
        d_rows = grad_padded[rows_source]
        pre_gate = jnp.dot(x_rows, gate_w, preferred_element_type=jnp.float32)
        pre_up = jnp.dot(x_rows, up_w, preferred_element_type=jnp.float32)
        activated = jax.nn.silu(pre_gate)
        hidden = (activated * pre_up).astype(jnp.bfloat16)
        outputs = jnp.dot(hidden, down_w.T, preferred_element_type=jnp.float32).astype(jnp.bfloat16)
        hidden_grad = jnp.dot(d_rows, down_w, preferred_element_type=jnp.float32)
        sigmoid_gate = jax.nn.sigmoid(pre_gate)
        gate_grad = (hidden_grad * pre_up * sigmoid_gate * (1.0 + pre_gate * (1.0 - sigmoid_gate))).astype(jnp.bfloat16)
        up_grad = (hidden_grad * activated).astype(jnp.bfloat16)
        input_part = (jnp.dot(gate_grad, gate_w.T, preferred_element_type=jnp.float32)
                      + jnp.dot(up_grad, up_w.T, preferred_element_type=jnp.float32)).astype(jnp.bfloat16)
        grad_gate_w = jnp.dot(x_rows.T, gate_grad, preferred_element_type=jnp.float32)
        grad_up_w = jnp.dot(x_rows.T, up_grad, preferred_element_type=jnp.float32)
        grad_down_w = jnp.dot(d_rows.T, hidden, preferred_element_type=jnp.float32)
        return outputs, input_part, grad_gate_w, grad_up_w, grad_down_w

    outputs_all, parts_all, grad_w_gate, grad_w_up, grad_w_down = lax.map(expert, (w_gate, w_up, w_down, source))
    expert_out = outputs_all[flat_routes, position].reshape(TOKENS, TOP, D).astype(jnp.float32)
    input_parts = parts_all[flat_routes, position].reshape(TOKENS, TOP, D).astype(jnp.float32)
    layer_out = jnp.sum(gates[:, :, None] * expert_out, axis=1).astype(jnp.bfloat16)
    grad_gates = jnp.sum(cotangent.astype(jnp.float32)[:, None, :] * expert_out, axis=-1)
    grad_input = jnp.sum(input_parts, axis=1).astype(jnp.bfloat16)
    return layer_out, grad_input, grad_gates, grad_w_gate, grad_w_up, grad_w_down
```

```python
import jax
import jax.numpy as jnp
from jax import lax
from jax.sharding import PartitionSpec as P

F32 = jnp.float32
BF16 = jnp.bfloat16


def dot(left, right, left_dim, right_dim):
    return lax.dot_general(
        left, right, (((left_dim,), (right_dim,)), ((), ())), preferred_element_type=F32
    )


def shards(checkpoint, cotangent, routes, gates, w_gate, w_up, w_down):
    tok_rows, features = cotangent.shape
    ep_size = lax.axis_size("ep")
    w_gate, w_up, w_down = w_gate[0], w_up[0], w_down[0]

    chosen = routes[:, :, None] == jnp.arange(ep_size, dtype=jnp.int32)[None, None, :]
    gate_table = jnp.sum(jnp.where(chosen, gates[:, :, None], 0.0), axis=1)
    gate = lax.all_to_all(gate_table.T, "ep", split_axis=0, concat_axis=0, tiled=True)
    gate = gate.reshape(ep_size * tok_rows, 1)
    cot = lax.all_gather(cotangent, "ep", axis=0, tiled=True)
    inputs = lax.all_to_all(checkpoint, "dp", split_axis=0, concat_axis=1, tiled=True)
    x = lax.all_gather(inputs, "ep", axis=0, tiled=True)

    hidden_back = dot(cot, w_down, 1, 0)
    pre_gate = dot(x, w_gate, 1, 0)
    pre_up = dot(x, w_up, 1, 0)
    sigmoid = jax.nn.sigmoid(pre_gate)
    activated = pre_gate * sigmoid
    hidden = activated * pre_up
    gated_hidden = (gate * hidden).astype(BF16)
    gate_dots = jnp.sum(hidden_back * hidden, axis=1)
    hidden_grad = gate * hidden_back
    gate_grad = (hidden_grad * pre_up * sigmoid * (1.0 + pre_gate * (1.0 - sigmoid))).astype(BF16)
    up_grad = (hidden_grad * activated).astype(BF16)

    def scattered(left, right):
        term = dot(left, right, 0, 0).astype(BF16)
        summed = lax.psum_scatter(term, "dp", scatter_dimension=0, tiled=True)
        return summed.astype(F32)[None]

    grad_w_down = scattered(cot, gated_hidden)
    grad_w_gate = scattered(x, gate_grad)
    grad_w_up = scattered(x, up_grad)

    def returned(rows):
        rows = rows.reshape(ep_size, tok_rows, -1)
        return lax.all_to_all(rows, "ep", split_axis=0, concat_axis=0, tiled=True)

    gate_dots = returned(gate_dots)[:, :, 0]
    out_part = returned(dot(gated_hidden, w_down, 1, 1).astype(BF16))
    in_part = returned((dot(gate_grad, w_gate, 1, 1) + dot(up_grad, w_up, 1, 1)).astype(BF16))
    layer_out = jnp.sum(out_part.astype(F32), axis=0).astype(BF16)
    grad_input = jnp.sum(in_part.astype(F32), axis=0).astype(BF16)
    grad_gates = jnp.sum(jnp.where(chosen, gate_dots.T[:, None, :], 0.0), axis=2)
    return (layer_out, grad_input, grad_gates, grad_w_gate, grad_w_up, grad_w_down)


def solution(mesh):
    tokens = P(("ep", "dp"), None)
    weights = P("ep", None, None)
    slices = P("ep", "dp", None)
    return jax.shard_map(
        shards,
        mesh=mesh,
        in_specs=(P("ep", "dp"), tokens, tokens, tokens, weights, weights, weights),
        out_specs=(tokens, tokens, tokens, slices, slices, slices),
        check_vma=False,
    )
```

```python
import functools

import jax
import jax.numpy as jnp
from jax import lax
from jax.experimental import pallas as pl
from jax.experimental.pallas import tpu as pltpu
from jax.sharding import PartitionSpec as P

F32 = jnp.float32
BF16 = jnp.bfloat16

MESH = pl.DeviceIdType.MESH
VMEM_BYTES = 56 * 1024 * 1024
LAG = 2


def remote(src, dst, send, recv, where):
    return pltpu.make_async_remote_copy(
        src_ref=src,
        dst_ref=dst,
        send_sem=send,
        recv_sem=recv,
        device_id=where,
        device_id_type=MESH,
    )


def dispatch_kernel(
    ep, dp, saved, cot, table, x_all, cot_all, table_all, own_sem, x_send, x_recv, e_send, e_recv
):
    me_ep, me_dp = lax.axis_index("ep"), lax.axis_index("dp")
    tok, width = cot.shape[0], saved.shape[1]
    barrier = pltpu.get_barrier_semaphore()
    for i in range(1, ep):
        pl.semaphore_signal(
            barrier, inc=1, device_id={"ep": lax.rem(me_ep + i, ep)}, device_id_type=MESH
        )
    for i in range(1, dp):
        pl.semaphore_signal(
            barrier, inc=1, device_id={"dp": lax.rem(me_dp + i, dp)}, device_id_type=MESH
        )
    pl.semaphore_wait(barrier, ep + dp - 2)

    def rows(index):
        return saved.at[pl.ds(pl.multiple_of(index * tok, tok), tok), :]

    columns = x_all.at[me_ep, :, pl.ds(pl.multiple_of(me_dp * width, width), width)]
    slices = []
    for i in range(1, dp):
        to = lax.rem(me_dp + i, dp)
        slices.append(remote(rows(to), columns, x_send.at[i], x_recv.at[i], {"dp": to}))
        slices[-1].start()
    blocks = []
    for a, (src, dst) in enumerate(((cot, cot_all), (table, table_all), (x_all, x_all))):
        for i in range(1, ep):
            to = lax.rem(me_ep + i, ep)
            part = src if a == 0 else src.at[to if a == 1 else me_ep]
            blocks.append(
                remote(part, dst.at[me_ep], e_send.at[a, i], e_recv.at[a, i], {"ep": to})
            )
            if a < 2:
                blocks[-1].start()
    local = [
        pltpu.make_async_copy(rows(me_dp), columns, own_sem.at[0]),
        pltpu.make_async_copy(cot, cot_all.at[me_ep], own_sem.at[1]),
        pltpu.make_async_copy(table.at[me_ep], table_all.at[me_ep], own_sem.at[2]),
    ]
    for copy in local:
        copy.start()
    local[0].wait()
    for copy in slices:
        copy.wait_recv()
    for copy in blocks[2 * (ep - 1) :]:
        copy.start()
    for copy in slices:
        copy.wait_send()
    local[1].wait()
    local[2].wait()
    for copy in blocks:
        copy.wait()


def dispatch(checkpoint, cotangent, table, ep, dp):
    tok, features = cotangent.shape
    anywhere = pl.BlockSpec(memory_space=pl.ANY)
    rows = jax.ShapeDtypeStruct((ep, tok, features), BF16)
    return pl.pallas_call(
        functools.partial(dispatch_kernel, ep, dp),
        out_shape=(rows, rows, jax.ShapeDtypeStruct(table.shape, F32)),
        in_specs=[anywhere] * 3,
        out_specs=(anywhere,) * 3,
        scratch_shapes=[
            pltpu.SemaphoreType.DMA((3,)),
            pltpu.SemaphoreType.DMA((dp,)),
            pltpu.SemaphoreType.DMA((dp,)),
            pltpu.SemaphoreType.DMA((3, ep)),
            pltpu.SemaphoreType.DMA((3, ep)),
        ],
        compiler_params=pltpu.CompilerParams(collective_id=0, has_side_effects=True),
    )(checkpoint, cotangent, table)


def combine_kernel(ep, dp, *refs):
    sent, terms, back, sums = refs[0:3], refs[3:6], refs[6:9], refs[9:12]
    own, core, right, left = refs[12:16]
    own_sem, ret_send, ret_recv, core_send, core_recv = refs[16:21]
    right_send, right_recv, left_send, left_recv = refs[21:25]
    me_ep, me_dp = lax.axis_index("ep"), lax.axis_index("dp")
    chips = dp // 2
    z, c = me_dp // 2, lax.rem(me_dp, 2)
    partner = {"dp": z * 2 + 1 - c}
    up, down = {"dp": me_dp + 2}, {"dp": me_dp - 2}
    not_last, not_first = z < chips - 1, z > 0

    loads = []
    for m in range(3):
        loads.append(pltpu.make_async_copy(terms[m], own.at[m], own_sem.at[m]))
        loads[-1].start()
    barrier = pltpu.get_barrier_semaphore()
    for i in range(1, ep):
        pl.semaphore_signal(
            barrier, inc=1, device_id={"ep": lax.rem(me_ep + i, ep)}, device_id_type=MESH
        )
    pl.semaphore_signal(barrier, inc=1, device_id=partner, device_id_type=MESH)

    @pl.when(not_last)
    def _():
        pl.semaphore_signal(barrier, inc=1, device_id=up, device_id_type=MESH)

    @pl.when(not_first)
    def _():
        pl.semaphore_signal(barrier, inc=1, device_id=down, device_id_type=MESH)

    pl.semaphore_wait(barrier, ep + not_last.astype(jnp.int32) + not_first.astype(jnp.int32))

    def core_copy(d, m):
        return remote(
            own.at[m, d * 2 + 1 - c], core.at[d, m], core_send.at[d, m], core_recv.at[d, m], partner
        )

    def right_copy(d, m):
        return remote(
            core.at[d, m], right.at[d, m], right_send.at[d, m], right_recv.at[d, m], up
        )

    def left_copy(d, m):
        return remote(core.at[d, m], left.at[d, m], left_send.at[d, m], left_recv.at[d, m], down)

    for copy in loads:
        copy.wait()
    lower = z < chips // 2
    for k in range(chips):
        for m in range(3):
            core_copy(jnp.where(lower, chips - 1 - k, k), m).start()

    returns = []
    for a in range(3):
        for i in range(1, ep):
            to = lax.rem(me_ep + i, ep)
            returns.append(
                remote(
                    sent[a].at[to],
                    back[a].at[me_ep],
                    ret_send.at[a, i],
                    ret_recv.at[a, i],
                    {"ep": to},
                )
            )
            returns[-1].start()
    keeps = [
        pltpu.make_async_copy(sent[a].at[me_ep], back[a].at[me_ep], own_sem.at[3 + a])
        for a in range(3)
    ]
    for copy in keeps:
        copy.start()

    steps = (chips - 1) * 3
    right_lag = jnp.where(lower, 0, LAG)
    left_lag = LAG - right_lag

    def step(i, carry):
        ir, il = i - right_lag, i - left_lag
        kr, mr = lax.div(jnp.maximum(ir, 0), 3), lax.rem(jnp.maximum(ir, 0), 3)
        kl, ml = lax.div(jnp.maximum(il, 0), 3), lax.rem(jnp.maximum(il, 0), 3)
        dr, dl = chips - 1 - kr, kl

        def forward(d, m, mine, arrived, copy_of, has):
            @pl.when(mine)
            def _():
                core_copy(d, m).wait_recv()

                @pl.when(has)
                def _():
                    copy_of(d, m).wait_recv()
                    core[d, m] = (
                        own[m, d * 2 + c].astype(F32)
                        + core[d, m].astype(F32)
                        + arrived[d, m].astype(F32)
                    ).astype(BF16)

                @pl.when(jnp.logical_not(has))
                def _():
                    core[d, m] = (
                        own[m, d * 2 + c].astype(F32) + core[d, m].astype(F32)
                    ).astype(BF16)

                copy_of(d, m).start()

        forward(dr, mr, (ir >= 0) & (ir < steps) & (dr > z), right, right_copy, not_first)
        forward(dl, ml, (il >= 0) & (il < steps) & (dl < z), left, left_copy, not_last)
        return carry

    lax.fori_loop(0, steps + LAG, step, 0)

    for m in range(3):
        core_copy(z, m).wait_recv()
        sums[m][...] = own[m, z * 2 + c].astype(F32) + core[z, m].astype(F32)

        @pl.when(not_first)
        def _():
            right_copy(z, m).wait_recv()
            sums[m][...] += right[z, m].astype(F32)

        @pl.when(not_last)
        def _():
            left_copy(z, m).wait_recv()
            sums[m][...] += left[z, m].astype(F32)

    for d in range(chips):
        for m in range(3):
            core_copy(d, m).wait_send()

            @pl.when(d > z)
            def _():
                right_copy(d, m).wait_send()

            @pl.when(d < z)
            def _():
                left_copy(d, m).wait_send()

    for copy in keeps + returns:
        copy.wait()


def combine(sent, terms, ep, dp):
    features, units = terms[0].shape
    rows, chips = features // dp, dp // 2
    anywhere = pl.BlockSpec(memory_space=pl.ANY)
    dma = pltpu.SemaphoreType.DMA
    slots = pltpu.VMEM((chips, 3, rows, units), BF16)
    return pl.pallas_call(
        functools.partial(combine_kernel, ep, dp),
        out_shape=[jax.ShapeDtypeStruct(a.shape, a.dtype) for a in sent]
        + [jax.ShapeDtypeStruct((rows, units), F32)] * 3,
        in_specs=[anywhere] * 6,
        out_specs=[anywhere] * 3 + [pl.BlockSpec(memory_space=pltpu.VMEM)] * 3,
        scratch_shapes=[pltpu.VMEM((3, dp, rows, units), BF16), slots, slots, slots, dma((6,))]
        + [dma((3, ep))] * 2
        + [dma((chips, 3))] * 6,
        compiler_params=pltpu.CompilerParams(
            collective_id=1, has_side_effects=True, vmem_limit_bytes=VMEM_BYTES
        ),
    )(*sent, *[term.reshape(dp, rows, units) for term in terms])


def dot(left, right, left_dim, right_dim):
    return lax.dot_general(
        left, right, (((left_dim,), (right_dim,)), ((), ())), preferred_element_type=F32
    )


def shards(checkpoint, cotangent, routes, gates, w_gate, w_up, w_down):
    tok_rows, features = cotangent.shape
    ep_size = lax.axis_size("ep")
    w_gate, w_up, w_down = w_gate[0], w_up[0], w_down[0]

    chosen = routes[:, :, None] == jnp.arange(ep_size, dtype=jnp.int32)[None, None, :]
    gate_table = jnp.sum(jnp.where(chosen, gates[:, :, None], 0.0), axis=1)
    table = jnp.broadcast_to(gate_table.T[:, None, :], (ep_size, 8, tok_rows))
    x, cot, table = dispatch(checkpoint, cotangent, table, ep_size, lax.axis_size("dp"))
    x, cot = (rows.reshape(ep_size * tok_rows, features) for rows in (x, cot))
    gate = table[:, 0, :].reshape(ep_size * tok_rows, 1)

    hidden_back = dot(cot, w_down, 1, 0)
    pre_gate = dot(x, w_gate, 1, 0)
    pre_up = dot(x, w_up, 1, 0)
    sigmoid = jax.nn.sigmoid(pre_gate)
    activated = pre_gate * sigmoid
    hidden = activated * pre_up
    gated_hidden = (gate * hidden).astype(BF16)
    gate_dots = jnp.sum(hidden_back * hidden, axis=1)
    hidden_grad = gate * hidden_back
    gate_grad = (hidden_grad * pre_up * sigmoid * (1.0 + pre_gate * (1.0 - sigmoid))).astype(BF16)
    up_grad = (hidden_grad * activated).astype(BF16)

    terms = [
        dot(left, right, 0, 0).astype(BF16)
        for left, right in ((x, gate_grad), (x, up_grad), (cot, gated_hidden))
    ]
    out_part = dot(gated_hidden, w_down, 1, 1).astype(BF16)
    in_part = (dot(gate_grad, w_gate, 1, 1) + dot(up_grad, w_up, 1, 1)).astype(BF16)
    out_part, in_part = (
        rows.reshape(ep_size, tok_rows, features) for rows in (out_part, in_part)
    )
    gate_dots = jnp.broadcast_to(
        gate_dots.reshape(ep_size, 1, tok_rows), (ep_size, 8, tok_rows)
    )
    out_part, in_part, gate_dots, grad_w_gate, grad_w_up, grad_w_down = combine(
        (out_part, in_part, gate_dots), terms, ep_size, lax.axis_size("dp")
    )
    gate_dots = gate_dots[:, 0, :]
    layer_out = jnp.sum(out_part.astype(F32), axis=0).astype(BF16)
    grad_input = jnp.sum(in_part.astype(F32), axis=0).astype(BF16)
    grad_gates = jnp.sum(jnp.where(chosen, gate_dots.T[:, None, :], 0.0), axis=2)
    return (
        layer_out,
        grad_input,
        grad_gates,
        grad_w_gate[None],
        grad_w_up[None],
        grad_w_down[None],
    )


def solution(mesh):
    tokens = P(("ep", "dp"), None)
    weights = P("ep", None, None)
    slices = P("ep", "dp", None)
    return jax.shard_map(
        shards,
        mesh=mesh,
        in_specs=(P("ep", "dp"), tokens, tokens, tokens, weights, weights, weights),
        out_specs=(tokens, tokens, tokens, slices, slices, slices),
        check_vma=False,
    )
```

```python
import functools

import jax
import jax.numpy as jnp
from jax import lax
from jax.experimental import pallas as pl
from jax.experimental.pallas import tpu as pltpu
from jax.sharding import PartitionSpec as P

F32 = jnp.float32
BF16 = jnp.bfloat16

MESH = pl.DeviceIdType.MESH
VMEM_BYTES = 56 * 1024 * 1024
LAG = 2


def remote(src, dst, send, recv, where):
    return pltpu.make_async_remote_copy(
        src_ref=src,
        dst_ref=dst,
        send_sem=send,
        recv_sem=recv,
        device_id=where,
        device_id_type=MESH,
    )


def dispatch_kernel(
    ep, dp, saved, cot, table, x_all, cot_all, table_all, own_sem, x_send, x_recv, e_send, e_recv
):
    me_ep, me_dp = lax.axis_index("ep"), lax.axis_index("dp")
    tok, width = cot.shape[0], saved.shape[1]
    barrier = pltpu.get_barrier_semaphore()
    for i in range(1, ep):
        pl.semaphore_signal(
            barrier, inc=1, device_id={"ep": lax.rem(me_ep + i, ep)}, device_id_type=MESH
        )
    for i in range(1, dp):
        pl.semaphore_signal(
            barrier, inc=1, device_id={"dp": lax.rem(me_dp + i, dp)}, device_id_type=MESH
        )
    pl.semaphore_wait(barrier, ep + dp - 2)

    def rows(index):
        return saved.at[pl.ds(pl.multiple_of(index * tok, tok), tok), :]

    columns = x_all.at[me_ep, :, pl.ds(pl.multiple_of(me_dp * width, width), width)]
    slices = []
    for i in range(1, dp):
        to = lax.rem(me_dp + i, dp)
        slices.append(remote(rows(to), columns, x_send.at[i], x_recv.at[i], {"dp": to}))
        slices[-1].start()
    blocks = []
    for a, (src, dst) in enumerate(((cot, cot_all), (table, table_all), (x_all, x_all))):
        for i in range(1, ep):
            to = lax.rem(me_ep + i, ep)
            part = src if a == 0 else src.at[to if a == 1 else me_ep]
            blocks.append(
                remote(part, dst.at[me_ep], e_send.at[a, i], e_recv.at[a, i], {"ep": to})
            )
            if a < 2:
                blocks[-1].start()
    local = [
        pltpu.make_async_copy(rows(me_dp), columns, own_sem.at[0]),
        pltpu.make_async_copy(cot, cot_all.at[me_ep], own_sem.at[1]),
        pltpu.make_async_copy(table.at[me_ep], table_all.at[me_ep], own_sem.at[2]),
    ]
    for copy in local:
        copy.start()
    local[0].wait()
    for copy in slices:
        copy.wait_recv()
    for copy in blocks[2 * (ep - 1) :]:
        copy.start()
    for copy in slices:
        copy.wait_send()
    local[1].wait()
    local[2].wait()
    for copy in blocks:
        copy.wait()


def dispatch(checkpoint, cotangent, table, ep, dp):
    tok, features = cotangent.shape
    anywhere = pl.BlockSpec(memory_space=pl.ANY)
    rows = jax.ShapeDtypeStruct((ep, tok, features), BF16)
    return pl.pallas_call(
        functools.partial(dispatch_kernel, ep, dp),
        out_shape=(rows, rows, jax.ShapeDtypeStruct(table.shape, F32)),
        in_specs=[anywhere] * 3,
        out_specs=(anywhere,) * 3,
        scratch_shapes=[
            pltpu.SemaphoreType.DMA((3,)),
            pltpu.SemaphoreType.DMA((dp,)),
            pltpu.SemaphoreType.DMA((dp,)),
            pltpu.SemaphoreType.DMA((3, ep)),
            pltpu.SemaphoreType.DMA((3, ep)),
        ],
        compiler_params=pltpu.CompilerParams(collective_id=0, has_side_effects=True),
    )(checkpoint, cotangent, table)


def combine_kernel(ep, dp, *refs):
    sent, terms, back, sums = refs[0:3], refs[3:6], refs[6:9], refs[9:12]
    own, core, right, left = refs[12:16]
    own_sem, ret_send, ret_recv, core_send, core_recv = refs[16:21]
    right_send, right_recv, left_send, left_recv = refs[21:25]
    me_ep, me_dp = lax.axis_index("ep"), lax.axis_index("dp")
    chips = dp // 2
    z, c = me_dp // 2, lax.rem(me_dp, 2)
    partner = {"dp": z * 2 + 1 - c}
    up, down = {"dp": me_dp + 2}, {"dp": me_dp - 2}
    not_last, not_first = z < chips - 1, z > 0

    loads = []
    for m in range(3):
        loads.append(pltpu.make_async_copy(terms[m], own.at[m], own_sem.at[m]))
        loads[-1].start()
    barrier = pltpu.get_barrier_semaphore()
    for i in range(1, ep):
        pl.semaphore_signal(
            barrier, inc=1, device_id={"ep": lax.rem(me_ep + i, ep)}, device_id_type=MESH
        )
    pl.semaphore_signal(barrier, inc=1, device_id=partner, device_id_type=MESH)

    @pl.when(not_last)
    def _():
        pl.semaphore_signal(barrier, inc=1, device_id=up, device_id_type=MESH)

    @pl.when(not_first)
    def _():
        pl.semaphore_signal(barrier, inc=1, device_id=down, device_id_type=MESH)

    pl.semaphore_wait(barrier, ep + not_last.astype(jnp.int32) + not_first.astype(jnp.int32))

    def core_copy(d, m):
        return remote(
            own.at[m, d * 2 + 1 - c], core.at[d, m], core_send.at[d, m], core_recv.at[d, m], partner
        )

    def right_copy(d, m):
        return remote(
            core.at[d, m], right.at[d, m], right_send.at[d, m], right_recv.at[d, m], up
        )

    def left_copy(d, m):
        return remote(core.at[d, m], left.at[d, m], left_send.at[d, m], left_recv.at[d, m], down)

    lower = z < chips // 2
    for k in range(chips):
        for m in range(3):
            if k == 0:
                loads[m].wait()
            core_copy(jnp.where(lower, chips - 1 - k, k), m).start()

    returns = []
    for a in range(3):
        for i in range(1, ep):
            to = lax.rem(me_ep + i, ep)
            returns.append(
                remote(
                    sent[a].at[to],
                    back[a].at[me_ep],
                    ret_send.at[a, i],
                    ret_recv.at[a, i],
                    {"ep": to},
                )
            )
            returns[-1].start()
    keeps = [
        pltpu.make_async_copy(sent[a].at[me_ep], back[a].at[me_ep], own_sem.at[3 + a])
        for a in range(3)
    ]
    for copy in keeps:
        copy.start()

    steps = (chips - 1) * 3
    right_lag = jnp.where(lower, 0, LAG)
    left_lag = LAG - right_lag

    def step(i, carry):
        ir, il = i - right_lag, i - left_lag
        kr, mr = lax.div(jnp.maximum(ir, 0), 3), lax.rem(jnp.maximum(ir, 0), 3)
        kl, ml = lax.div(jnp.maximum(il, 0), 3), lax.rem(jnp.maximum(il, 0), 3)
        dr, dl = chips - 1 - kr, kl

        def forward(d, m, mine, arrived, copy_of, has):
            @pl.when(mine)
            def _():
                core_copy(d, m).wait_recv()

                @pl.when(has)
                def _():
                    copy_of(d, m).wait_recv()
                    core[d, m] = (
                        own[m, d * 2 + c].astype(F32)
                        + core[d, m].astype(F32)
                        + arrived[d, m].astype(F32)
                    ).astype(BF16)

                @pl.when(jnp.logical_not(has))
                def _():
                    core[d, m] = (
                        own[m, d * 2 + c].astype(F32) + core[d, m].astype(F32)
                    ).astype(BF16)

                copy_of(d, m).start()

        forward(dr, mr, (ir >= 0) & (ir < steps) & (dr > z), right, right_copy, not_first)
        forward(dl, ml, (il >= 0) & (il < steps) & (dl < z), left, left_copy, not_last)
        return carry

    lax.fori_loop(0, steps + LAG, step, 0)

    for m in range(3):
        core_copy(z, m).wait_recv()
        sums[m][...] = own[m, z * 2 + c].astype(F32) + core[z, m].astype(F32)

        @pl.when(not_first)
        def _():
            right_copy(z, m).wait_recv()
            sums[m][...] += right[z, m].astype(F32)

        @pl.when(not_last)
        def _():
            left_copy(z, m).wait_recv()
            sums[m][...] += left[z, m].astype(F32)

    for d in range(chips):
        for m in range(3):
            core_copy(d, m).wait_send()

            @pl.when(d > z)
            def _():
                right_copy(d, m).wait_send()

            @pl.when(d < z)
            def _():
                left_copy(d, m).wait_send()

    for copy in keeps + returns:
        copy.wait()


def combine(sent, terms, ep, dp):
    features, units = terms[0].shape
    rows, chips = features // dp, dp // 2
    anywhere = pl.BlockSpec(memory_space=pl.ANY)
    dma = pltpu.SemaphoreType.DMA
    slots = pltpu.VMEM((chips, 3, rows, units), BF16)
    return pl.pallas_call(
        functools.partial(combine_kernel, ep, dp),
        out_shape=[jax.ShapeDtypeStruct(a.shape, a.dtype) for a in sent]
        + [jax.ShapeDtypeStruct((rows, units), F32)] * 3,
        in_specs=[anywhere] * 6,
        out_specs=[anywhere] * 3 + [pl.BlockSpec(memory_space=pltpu.VMEM)] * 3,
        scratch_shapes=[pltpu.VMEM((3, dp, rows, units), BF16), slots, slots, slots, dma((6,))]
        + [dma((3, ep))] * 2
        + [dma((chips, 3))] * 6,
        compiler_params=pltpu.CompilerParams(
            collective_id=1, has_side_effects=True, vmem_limit_bytes=VMEM_BYTES
        ),
    )(*sent, *[term.reshape(dp, rows, units) for term in terms])


def dot(left, right, left_dim, right_dim):
    return lax.dot_general(
        left, right, (((left_dim,), (right_dim,)), ((), ())), preferred_element_type=F32
    )


def shards(checkpoint, cotangent, routes, gates, w_gate, w_up, w_down):
    tok_rows, features = cotangent.shape
    ep_size = lax.axis_size("ep")
    w_gate, w_up, w_down = w_gate[0], w_up[0], w_down[0]

    chosen = routes[:, :, None] == jnp.arange(ep_size, dtype=jnp.int32)[None, None, :]
    gate_table = jnp.sum(jnp.where(chosen, gates[:, :, None], 0.0), axis=1)
    table = jnp.broadcast_to(gate_table.T[:, None, :], (ep_size, 8, tok_rows))
    x, cot, table = dispatch(checkpoint, cotangent, table, ep_size, lax.axis_size("dp"))
    x, cot = (rows.reshape(ep_size * tok_rows, features) for rows in (x, cot))
    gate = table[:, 0, :].reshape(ep_size * tok_rows, 1)

    hidden_back = dot(cot, w_down, 1, 0)
    pre_gate = dot(x, w_gate, 1, 0)
    pre_up = dot(x, w_up, 1, 0)
    sigmoid = jax.nn.sigmoid(pre_gate)
    activated = pre_gate * sigmoid
    hidden = activated * pre_up
    gated_hidden = (gate * hidden).astype(BF16)
    gate_dots = jnp.sum(hidden_back * hidden, axis=1)
    hidden_grad = gate * hidden_back
    gate_grad = (hidden_grad * pre_up * sigmoid * (1.0 + pre_gate * (1.0 - sigmoid))).astype(BF16)
    up_grad = (hidden_grad * activated).astype(BF16)

    terms = [
        dot(left, right, 0, 0).astype(BF16)
        for left, right in ((x, gate_grad), (x, up_grad), (cot, gated_hidden))
    ]
    out_part = dot(gated_hidden, w_down, 1, 1).astype(BF16)
    in_part = (dot(gate_grad, w_gate, 1, 1) + dot(up_grad, w_up, 1, 1)).astype(BF16)
    out_part, in_part = (
        rows.reshape(ep_size, tok_rows, features) for rows in (out_part, in_part)
    )
    gate_dots = jnp.broadcast_to(
        gate_dots.reshape(ep_size, 1, tok_rows), (ep_size, 8, tok_rows)
    )
    out_part, in_part, gate_dots, grad_w_gate, grad_w_up, grad_w_down = combine(
        (out_part, in_part, gate_dots), terms, ep_size, lax.axis_size("dp")
    )
    gate_dots = gate_dots[:, 0, :]
    layer_out = jnp.sum(out_part.astype(F32), axis=0).astype(BF16)
    grad_input = jnp.sum(in_part.astype(F32), axis=0).astype(BF16)
    grad_gates = jnp.sum(jnp.where(chosen, gate_dots.T[:, None, :], 0.0), axis=2)
    return (
        layer_out,
        grad_input,
        grad_gates,
        grad_w_gate[None],
        grad_w_up[None],
        grad_w_down[None],
    )


def solution(mesh):
    tokens = P(("ep", "dp"), None)
    weights = P("ep", None, None)
    slices = P("ep", "dp", None)
    return jax.shard_map(
        shards,
        mesh=mesh,
        in_specs=(P("ep", "dp"), tokens, tokens, tokens, weights, weights, weights),
        out_specs=(tokens, tokens, tokens, slices, slices, slices),
        check_vma=False,
    )
```
